32 devices in a mesh: ctx: 16 (over z, x, core), head: 2 (over y).
Axes of the slice: x: 2, y: 2, z: 4, core: 2. Of those that a mesh axis runs over, the one named last changes fastest.
Arguments:
- queries: bfloat16 [8192, 8192], P('ctx', 'head'), may hold values from -128 to 128
- key_rows: bfloat16 [8192, 1024], P(('ctx', 'head')), may hold values from -8 to 8
- value_rows: bfloat16 [8192, 1024], P(('ctx', 'head')), may hold values from -6 to 6
- grad_output: bfloat16 [8192, 8192], P('ctx', 'head'), may hold values from -6 to 6
- doc_lengths: int32 [32], replicated, may hold values from 1 to 512, 8192 in all
Outputs:
- grad_queries: bfloat16 [8192, 8192], P('ctx', 'head')
- grad_keys: bfloat16 [8192, 1024], P(('ctx', 'head'))
- grad_values: bfloat16 [8192, 1024], P(('ctx', 'head'))
The draws below stay inside these ranges and needn't reach their ends.
Inputs may be any that keep to these rules, and one draw needn't show every extreme that they name: `doc_lengths`: document lengths sum to 8192; the longest is exactly 512.
All inputs are finite; a program needn't handle non-finite values.
Results may differ from the reference program's by a relative error of at most 0.02.
Values may be sent and summed in bfloat16 or wider, within the bound.
No kernel may reach another device: no remote copies, remote signals or barrier semaphores. Data moves between devices by JAX's collectives and lax.ppermute only.
A program may use at most 256 MiB of HBM per device.

```python
import math
import jax
import jax.numpy as jnp
import numpy as np
from jax import lax

H = 64
KVH = 8
HD = 128
TOK_DEV = 512
TOKENS = 8192
NDOCS = 32


def base_keys(key):
    normal = jax.random.normal(jax.random.fold_in(key, 7), (TOKENS, KVH * HD), jnp.float32)
    return normal


def draw_key_rows(key, part):
    return base_keys(key).astype(jnp.bfloat16)


def draw_queries(key, part):
    normal = jax.random.normal(jax.random.fold_in(key, 11), (TOKENS, H * HD), jnp.float32)
    return normal.astype(jnp.bfloat16)


def levels(stream_key, extent, split, least, high):
    loudness = 1.0
    for position, shards_of in split:
        heights = jax.random.uniform(jax.random.fold_in(jax.random.fold_in(stream_key, 6), position), (shards_of,), jnp.float32, least / len(split), high / len(split))
        loudness = loudness * jnp.repeat(jnp.exp(heights), extent[position] // shards_of).reshape((-1,) + (1,) * (len(extent) - 1 - position))
    return loudness


def length_profile(count, total, bound, skew):
    portions = [(1 << 20) // math.isqrt(standing ** skew) + 1 for standing in range(2, count + 1)]
    surplus, holding = total - bound - (count - 1), [1] * (count - 1)
    while surplus > 0:
        candidates = [i for i in range(count - 1) if holding[i] < bound]
        mass, remaining = sum([portions[i] for i in candidates]), surplus
        for i in candidates:
            addition = min(bound - holding[i], max(1, remaining * portions[i] // mass), surplus)
            holding[i] = holding[i] + addition
            surplus = surplus - addition
    return np.array([bound] + holding)


def ragged(key, count, total, bound, slope):
    if count == 2:
        one = jax.random.randint(key, (), max(1, total - bound), min(bound, total - 1) + 1)
        return jnp.stack([one, total - one])
    tallies = jnp.asarray(length_profile(count, total, bound, slope), jnp.int32)
    pairs = (count - 1) // 2
    giver, sink = tallies[1:1 + 2 * pairs:2], tallies[2:2 + 2 * pairs:2]
    slack = jnp.minimum(giver - 1, bound - sink)
    passed = jax.random.randint(jax.random.fold_in(key, 1), (pairs,), 0, 1 << 20) % (slack + 1)
    tallies = tallies.at[1:1 + 2 * pairs:2].set(giver - passed).at[2:2 + 2 * pairs:2].set(sink + passed)
    return tallies[jax.random.permutation(jax.random.fold_in(key, 2), count)]


def normal_values(rng, dims, spread, reach, cuts=(), held_as=jnp.bfloat16):
    factor_of = levels(rng, dims, cuts, -0.22, 0.18) if cuts else 1.0
    entries = jax.random.normal(rng, dims, jnp.float32) * spread * factor_of
    return jnp.minimum(jnp.maximum(entries, -reach), reach).astype(held_as)


def setup_inputs(seed: int = 0) -> dict:
    splits = jax.random.split(jax.random.key(seed), 6)
    queries = draw_queries(jax.random.fold_in(splits[5], 71), 0)
    key_rows = draw_key_rows(jax.random.fold_in(splits[5], 71), 0)
    value_rows = normal_values(splits[2], (TOKENS, KVH * HD), 1.0, 6.0, ((0, 32),))
    grad_output = normal_values(splits[3], (TOKENS, H * HD), 1.0, 6.0, ((0, 16), (1, 2)))
    doc_lengths = ragged(splits[4], NDOCS, TOKENS, TOK_DEV, 1).astype(jnp.int32)
    return dict(queries=queries, key_rows=key_rows, value_rows=value_rows, grad_output=grad_output, doc_lengths=doc_lengths)


def rounded(value):
    return lax.optimization_barrier(value.astype(jnp.bfloat16)).astype(jnp.float32)

def reference(queries, key_rows, value_rows, grad_output, doc_lengths):
    groups = H // KVH
    factor = 1.0 / math.sqrt(HD)
    bounds = jnp.cumsum(doc_lengths).astype(jnp.int32)
    places = jnp.arange(TOKENS, dtype=jnp.int32)
    segment = lax.optimization_barrier(jnp.sum((places[:, None] >= bounds[None, :]).astype(jnp.int32), axis=1)).astype(jnp.int32)
    pad_seg = jnp.concatenate([jnp.full((TOK_DEV,), -1, jnp.int32), segment])
    pad_pos = jnp.concatenate([jnp.arange(TOK_DEV, dtype=jnp.int32) - TOK_DEV, places])
    key_pad = jnp.concatenate([jnp.zeros((TOK_DEV, KVH * HD), key_rows.dtype), key_rows]).reshape(TOKENS + TOK_DEV, KVH, HD)
    val_pad = jnp.concatenate([jnp.zeros((TOK_DEV, KVH * HD), value_rows.dtype), value_rows]).reshape(TOKENS + TOK_DEV, KVH, HD)
    query_all = queries.reshape(TOKENS, KVH, groups, HD)
    grad_all = grad_output.reshape(TOKENS, KVH, groups, HD)

    def one_block(accumulators, block_index):
        key_acc, val_acc = accumulators
        offset = (block_index * TOK_DEV).astype(jnp.int32)
        query_blk = lax.dynamic_slice_in_dim(query_all, offset, TOK_DEV, 0).astype(jnp.float32)
        grad_blk = lax.dynamic_slice_in_dim(grad_all, offset, TOK_DEV, 0).astype(jnp.float32)
        key_win = lax.dynamic_slice_in_dim(key_pad, offset, 2 * TOK_DEV, 0).astype(jnp.float32)
        val_win = lax.dynamic_slice_in_dim(val_pad, offset, 2 * TOK_DEV, 0).astype(jnp.float32)
        row_seg = lax.dynamic_slice_in_dim(segment, offset, TOK_DEV, 0)
        row_pos = lax.dynamic_slice_in_dim(places, offset, TOK_DEV, 0)
        col_seg = lax.dynamic_slice_in_dim(pad_seg, offset, 2 * TOK_DEV, 0)
        col_pos = lax.dynamic_slice_in_dim(pad_pos, offset, 2 * TOK_DEV, 0)
        allowed = (row_seg[:, None] == col_seg[None, :]) & (col_pos[None, :] <= row_pos[:, None])
        logits = jnp.einsum('rkgd,wkd->kgrw', query_blk, key_win) * factor
        logits = jnp.where(allowed[None, None], logits, -1e+30)
        maximum = lax.optimization_barrier(jnp.max(logits, axis=-1, keepdims=True))
        raised = jnp.exp(logits - maximum)
        weights = raised / lax.optimization_barrier(jnp.sum(raised, axis=-1, keepdims=True))
        weights_low = rounded(weights)
        output = rounded(jnp.einsum('kgrw,wkd->rkgd', weights_low, val_win))
        grad_weights = jnp.einsum('rkgd,wkd->kgrw', grad_blk, val_win)
        deltas = jnp.transpose(lax.optimization_barrier(jnp.sum(grad_blk * output, axis=-1)), (1, 2, 0))[..., None]
        grad_logits = rounded(weights * (grad_weights - deltas))
        grad_query = jnp.einsum('kgrw,wkd->rkgd', grad_logits, key_win) * factor
        grad_key = jnp.einsum('kgrw,rkgd->wkd', grad_logits, query_blk) * factor
        grad_val = jnp.einsum('kgrw,rkgd->wkd', weights_low, grad_blk)
        key_acc = lax.dynamic_update_slice_in_dim(key_acc, lax.dynamic_slice_in_dim(key_acc, offset, 2 * TOK_DEV, 0) + grad_key, offset, 0)
        val_acc = lax.dynamic_update_slice_in_dim(val_acc, lax.dynamic_slice_in_dim(val_acc, offset, 2 * TOK_DEV, 0) + grad_val, offset, 0)
        return ((key_acc, val_acc), grad_query.reshape(TOK_DEV, H * HD).astype(jnp.bfloat16))
    zeros = jnp.zeros((TOKENS + TOK_DEV, KVH, HD), jnp.float32)
    (key_acc, val_acc), grad_blocks = lax.scan(one_block, (zeros, zeros), jnp.arange(TOKENS // TOK_DEV, dtype=jnp.int32))
    grad_queries = grad_blocks.reshape(TOKENS, H * HD)
    grad_keys = key_acc[TOK_DEV:].reshape(TOKENS, KVH * HD).astype(jnp.bfloat16)
    grad_values = val_acc[TOK_DEV:].reshape(TOKENS, KVH * HD).astype(jnp.bfloat16)
    return (grad_queries, grad_keys, grad_values)
```

```python
import functools
import math

import jax
import jax.numpy as jnp
from jax import lax
from jax.experimental import pallas as pl
from jax.experimental.pallas import tpu as pltpu
from jax.sharding import PartitionSpec as P

H = 64
KVH = 8
HD = 128
G = H // KVH
NEG = -1e30
ROW_TILE = 128
HEADS_STEP = 2
BF16 = jnp.bfloat16
F32 = jnp.float32
NT = (((1,), (1,)), ((), ()))
NN = (((1,), (0,)), ((), ()))
TN = (((0,), (0,)), ((), ()))


def attn_kernel(info_ref, docs_ref, q_ref, do_ref, *refs, tokens, pieces, aliased):
    count = 2 * pieces
    k_in, v_in, refs = refs[:count], refs[count : 2 * count], refs[2 * count :]
    if aliased:
        refs = refs[1:]
    dq_ref, refs = refs[0], refs[1:]
    dk_out, dv_out, refs = refs[:count], refs[count : 2 * count], refs[2 * count :]
    k_win, v_win, dk_acc, dv_acc, bias, tiles = refs
    rt = ROW_TILE
    n_tiles = tokens // rt
    part = tokens // pieces
    scale = math.log2(math.e) / math.sqrt(HD)
    factor = 1.0 / math.sqrt(HD)
    base = info_ref[0] * tokens
    first_off = pl.multiple_of(info_ref[1], part)
    if pieces == 1:
        places = [0, tokens]
    else:
        second_off = pl.multiple_of(part - first_off, part)
        places = [first_off, second_off, tokens + first_off, tokens + second_off]

    @pl.when(pl.program_id(0) == 0)
    def _():
        pos = base + lax.broadcasted_iota(jnp.int32, (1, tokens), 1)

        def doc(i, carry):
            bound, start, firsts = carry
            bound = bound + docs_ref[i]
            start = jnp.where(pos >= bound, bound, start)
            firsts = tuple(
                jnp.where(base + r * rt >= bound, bound, f) for r, f in enumerate(firsts)
            )
            return bound, start, firsts

        zero = jnp.int32(0)
        _, start, firsts = lax.fori_loop(
            0, docs_ref.shape[0], doc, (zero, jnp.zeros((1, tokens), jnp.int32), (zero,) * n_tiles)
        )
        for r in range(n_tiles):
            tiles[r] = lax.div(base + (r + 1) * rt - 1 - firsts[r], rt) + 1
            key_pos = (
                base + r * rt - tokens + lax.broadcasted_iota(jnp.int32, (tokens + rt, rt), 0)
            )
            cols = slice(r * rt, (r + 1) * rt)
            ok = (key_pos >= start[:, cols]) & (key_pos <= pos[:, cols])
            bias[r] = jnp.where(ok, 0.0, NEG).astype(F32)

    for place, k, v in zip(places, k_in, v_in):
        k_win[pl.ds(place, part), :] = k[...]
        v_win[pl.ds(place, part), :] = v[...]
    dk_acc[...] = jnp.zeros_like(dk_acc)
    dv_acc[...] = jnp.zeros_like(dv_acc)

    def row_tile(r, _):
        row0 = pl.multiple_of(r * rt, rt)
        for n in range(1, n_tiles + 2):

            @pl.when(tiles[r] == n)
            def _(n=n):
                span = n * rt
                k0 = pl.multiple_of(tokens + row0 + rt - span, rt)
                k = k_win[pl.ds(k0, span), :]
                v = v_win[pl.ds(k0, span), :]
                mask = jnp.concatenate([bias[r, tokens + rt - span :, :]] * HEADS_STEP, axis=1)
                dk = dv = None
                for h in range(0, G, HEADS_STEP):
                    heads = [slice((h + i) * HD, (h + i + 1) * HD) for i in range(HEADS_STEP)]
                    rows = pl.ds(row0, rt)
                    q = jnp.concatenate([q_ref[rows, s] for s in heads], axis=0)
                    do = jnp.concatenate([do_ref[rows, s] for s in heads], axis=0)
                    s = lax.dot_general(k, q, NT, preferred_element_type=F32) + mask
                    dp = lax.dot_general(v, do, NT, preferred_element_type=F32)
                    e = jnp.exp2((s - jnp.max(s, axis=0, keepdims=True)) * scale)
                    inv = 1.0 / jnp.sum(e, axis=0, keepdims=True)
                    delta = jnp.sum(e * dp, axis=0, keepdims=True) * inv
                    p = e * inv
                    ds = (p * (dp - delta)).astype(BF16)
                    dv_h = lax.dot_general(p.astype(BF16), do, NN, preferred_element_type=F32)
                    dk_h = lax.dot_general(ds, q, NN, preferred_element_type=F32)
                    dk = dk_h if dk is None else dk + dk_h
                    dv = dv_h if dv is None else dv + dv_h
                    dq = lax.dot_general(ds, k, TN, preferred_element_type=F32)
                    dq = (dq * factor).astype(BF16)
                    for i, s in enumerate(heads):
                        dq_ref[rows, s] = dq[i * rt : (i + 1) * rt]
                dk_acc[pl.ds(k0, span), :] += dk
                dv_acc[pl.ds(k0, span), :] += dv

        return 0

    lax.fori_loop(0, n_tiles, row_tile, 0)
    for place, dk, dv in zip(places, dk_out, dv_out):
        dk[...] = (dk_acc[pl.ds(place, part), :] * factor).astype(dk.dtype)
        dv[...] = dv_acc[pl.ds(place, part), :].astype(dv.dtype)


def attention(info, docs, queries, grad_output, prev, own, grad_queries, chunk):
    tokens = queries.shape[0]
    pieces = len(own)
    part = tokens // pieces
    width = own[0].shape[1] // 2
    heads = width // HD
    first = chunk * heads
    wide = pl.BlockSpec((tokens, G * HD), lambda k: (0, first + k))
    key_block = pl.BlockSpec((part, HD), lambda k: (0, k))
    val_block = pl.BlockSpec((part, HD), lambda k: (0, heads + k))
    scalars = pl.BlockSpec(memory_space=pltpu.SMEM)
    count = 2 * pieces
    aliased = grad_queries is not None
    narrow = [jax.ShapeDtypeStruct((part, width), BF16)] * pieces + [
        jax.ShapeDtypeStruct((part, width), F32)
    ] * pieces
    work = 2 * tokens * G * HD * tokens * heads
    outs = pl.pallas_call(
        functools.partial(attn_kernel, tokens=tokens, pieces=pieces, aliased=aliased),
        grid=(heads,),
        in_specs=[scalars, scalars, wide, wide]
        + [key_block] * count
        + [val_block] * count
        + ([pl.BlockSpec(memory_space=pl.ANY)] if aliased else []),
        out_specs=[wide] + [key_block] * (2 * count),
        out_shape=[jax.ShapeDtypeStruct(queries.shape, BF16)] + narrow + narrow,
        scratch_shapes=[pltpu.VMEM((2 * tokens, HD), BF16)] * 2
        + [pltpu.VMEM((2 * tokens, HD), F32)] * 2
        + [
            pltpu.VMEM((tokens // ROW_TILE, tokens + ROW_TILE, ROW_TILE), F32),
            pltpu.SMEM((tokens // ROW_TILE,), jnp.int32),
        ],
        input_output_aliases={4 + 2 * count: 0} if aliased else {},
        compiler_params=pltpu.CompilerParams(vmem_limit_bytes=40 << 20),
        cost_estimate=pl.CostEstimate(
            flops=5 * work, bytes_accessed=3 * tokens * G * HD * 2 * heads, transcendentals=0
        ),
        name="attention",
    )(info, docs, queries, grad_output, *(prev + own) * 2, *([grad_queries] if aliased else []))
    dq, rest = outs[0], outs[1:]
    dk, dv = rest[:count], rest[count:]
    join = lambda i: jnp.concatenate([dk[i], dv[i]], axis=1)
    pair = lambda i: (dk[i], dv[i])
    return dq, [join(i) for i in range(pieces)], [pair(i) for i in range(pieces, count)]


def shift(value, steps):
    count = lax.axis_size("ctx")
    first, last = max(0, -steps), min(count, count - steps)
    return lax.ppermute(value, "ctx", [(i, i + steps) for i in range(first, last)])


def swap(value):
    return lax.ppermute(value, "head", [(0, 1), (1, 0)])


def add(own, arrived):
    return (jnp.concatenate(own, axis=1) + arrived.astype(F32)).astype(BF16)


def per_device(queries, key_rows, value_rows, grad_output, doc_lengths):
    tokens = queries.shape[0]
    head_count = lax.axis_size("head")
    kv_local = KVH // head_count
    local = kv_local * HD
    me = lax.axis_index("head")
    shard = lax.axis_index("ctx")
    chunks = 2 if kv_local % 2 == 0 else 1
    width = local // chunks
    cut = lambda x, start: lax.dynamic_slice_in_dim(x, start, width, axis=1)
    grad_queries = None

    if head_count == 2:
        info = jnp.stack([shard, me * (tokens // 2)]).astype(jnp.int32)
        both = lambda start: jnp.concatenate([cut(key_rows, start), cut(value_rows, start)], axis=1)
        mine = [both(me * local + j * width) for j in range(chunks)]
        recv = [swap(both((1 - me) * local + j * width)) for j in range(chunks)]
        prev = [[shift(mine[j], 1), shift(recv[j], 1)] for j in range(chunks)]
        kept, taken = [], []
        for j in range(chunks):
            grad_queries, gone, own = attention(
                info, doc_lengths, queries, grad_output, prev[j], [mine[j], recv[j]], grad_queries, j
            )
            taken.append(swap(add(own[1], shift(gone[1], -1))))
            kept.append(add(own[0], shift(gone[0], -1)))
        outs = []
        for at in range(2):
            here = [x[:, at * width : (at + 1) * width] for x in kept]
            there = [x[:, at * width : (at + 1) * width] for x in taken]
            low = jnp.concatenate([jnp.where(me == 0, a, b) for a, b in zip(here, there)], axis=1)
            high = jnp.concatenate([jnp.where(me == 0, b, a) for a, b in zip(here, there)], axis=1)
            outs.append(jnp.concatenate([low, high], axis=1))
        return (grad_queries, *outs)

    info = jnp.stack([shard, 0 * shard]).astype(jnp.int32)
    key_own = lax.all_to_all(key_rows, "head", split_axis=1, concat_axis=0, tiled=True)
    val_own = lax.all_to_all(value_rows, "head", split_axis=1, concat_axis=0, tiled=True)
    totals = []
    for j in range(chunks):
        own = jnp.concatenate([cut(key_own, j * width), cut(val_own, j * width)], axis=1)
        grad_queries, gone, mine = attention(
            info, doc_lengths, queries, grad_output, [shift(own, 1)], [own], grad_queries, j
        )
        totals.append(add(mine[0], shift(gone[0], -1)))
    outs = []
    for at in range(2):
        total = jnp.concatenate([x[:, at * width : (at + 1) * width] for x in totals], axis=1)
        outs.append(lax.all_to_all(total, "head", split_axis=0, concat_axis=1, tiled=True))
    return (grad_queries, *outs)


def solution(mesh):
    in_specs = (
        P("ctx", "head"),
        P(("ctx", "head"), None),
        P(("ctx", "head"), None),
        P("ctx", "head"),
        P(),
    )
    out_specs = (P("ctx", "head"), P(("ctx", "head"), None), P(("ctx", "head"), None))
    return jax.shard_map(
        per_device, mesh=mesh, in_specs=in_specs, out_specs=out_specs, check_vma=False
    )
```

```python
import functools
import math

import jax
import jax.numpy as jnp
from jax import lax
from jax.experimental import pallas as pl
from jax.experimental.pallas import tpu as pltpu
from jax.sharding import PartitionSpec as P

H = 64
KVH = 8
HD = 128
G = H // KVH
NEG = -1e30
ROW_TILE = 128
HEADS_STEP = 8
BF16 = jnp.bfloat16
F32 = jnp.float32
NT = (((1,), (1,)), ((), ()))
NN = (((1,), (0,)), ((), ()))
TN = (((0,), (0,)), ((), ()))


def attn_kernel(info_ref, docs_ref, q_ref, do_ref, *refs, tokens, pieces, aliased):
    count = 2 * pieces
    k_in, v_in, refs = refs[:count], refs[count : 2 * count], refs[2 * count :]
    if aliased:
        refs = refs[1:]
    dq_ref, refs = refs[0], refs[1:]
    dk_out, dv_out, refs = refs[:count], refs[count : 2 * count], refs[2 * count :]
    k_win, v_win, dk_acc, dv_acc, bias, tiles = refs
    rt = ROW_TILE
    n_tiles = tokens // rt
    part = tokens // pieces
    scale = math.log2(math.e) / math.sqrt(HD)
    factor = 1.0 / math.sqrt(HD)
    base = info_ref[0] * tokens
    first_off = pl.multiple_of(info_ref[1], part)
    if pieces == 1:
        places = [0, tokens]
    else:
        second_off = pl.multiple_of(part - first_off, part)
        places = [first_off, second_off, tokens + first_off, tokens + second_off]

    @pl.when(pl.program_id(0) == 0)
    def _():
        pos = base + lax.broadcasted_iota(jnp.int32, (1, tokens), 1)

        def doc(i, carry):
            bound, start, firsts = carry
            bound = bound + docs_ref[i]
            start = jnp.where(pos >= bound, bound, start)
            firsts = tuple(
                jnp.where(base + r * rt >= bound, bound, f) for r, f in enumerate(firsts)
            )
            return bound, start, firsts

        zero = jnp.int32(0)
        _, start, firsts = lax.fori_loop(
            0, docs_ref.shape[0], doc, (zero, jnp.zeros((1, tokens), jnp.int32), (zero,) * n_tiles)
        )
        for r in range(n_tiles):
            tiles[r] = lax.div(base + (r + 1) * rt - 1 - firsts[r], rt) + 1
            key_pos = (
                base + r * rt - tokens + lax.broadcasted_iota(jnp.int32, (tokens + rt, rt), 0)
            )
            cols = slice(r * rt, (r + 1) * rt)
            ok = (key_pos >= start[:, cols]) & (key_pos <= pos[:, cols])
            bias[r] = jnp.where(ok, 0.0, NEG).astype(F32)

    for place, k, v in zip(places, k_in, v_in):
        k_win[pl.ds(place, part), :] = k[...]
        v_win[pl.ds(place, part), :] = v[...]
    dk_acc[...] = jnp.zeros_like(dk_acc)
    dv_acc[...] = jnp.zeros_like(dv_acc)

    def row_tile(r, _):
        row0 = pl.multiple_of(r * rt, rt)
        for n in range(1, n_tiles + 2):

            @pl.when(tiles[r] == n)
            def _(n=n):
                span = n * rt
                k0 = pl.multiple_of(tokens + row0 + rt - span, rt)
                k = k_win[pl.ds(k0, span), :]
                v = v_win[pl.ds(k0, span), :]
                mask = jnp.concatenate([bias[r, tokens + rt - span :, :]] * HEADS_STEP, axis=1)
                dk = dv = None
                for h in range(0, G, HEADS_STEP):
                    heads = [slice((h + i) * HD, (h + i + 1) * HD) for i in range(HEADS_STEP)]
                    rows = pl.ds(row0, rt)
                    q = jnp.concatenate([q_ref[rows, s] for s in heads], axis=0)
                    do = jnp.concatenate([do_ref[rows, s] for s in heads], axis=0)
                    s = lax.dot_general(k, q, NT, preferred_element_type=F32) + mask
                    dp = lax.dot_general(v, do, NT, preferred_element_type=F32)
                    e = jnp.exp2((s - jnp.max(s, axis=0, keepdims=True)) * scale)
                    inv = 1.0 / jnp.sum(e, axis=0, keepdims=True)
                    delta = jnp.sum(e * dp, axis=0, keepdims=True) * inv
                    p = e * inv
                    ds = (p * (dp - delta)).astype(BF16)
                    dv_h = lax.dot_general(p.astype(BF16), do, NN, preferred_element_type=F32)
                    dk_h = lax.dot_general(ds, q, NN, preferred_element_type=F32)
                    dk = dk_h if dk is None else dk + dk_h
                    dv = dv_h if dv is None else dv + dv_h
                    dq = lax.dot_general(ds, k, TN, preferred_element_type=F32)
                    dq = (dq * factor).astype(BF16)
                    for i, s in enumerate(heads):
                        dq_ref[rows, s] = dq[i * rt : (i + 1) * rt]
                dk_acc[pl.ds(k0, span), :] += dk
                dv_acc[pl.ds(k0, span), :] += dv

        return 0

    lax.fori_loop(0, n_tiles, row_tile, 0)
    for place, dk, dv in zip(places, dk_out, dv_out):
        dk[...] = (dk_acc[pl.ds(place, part), :] * factor).astype(dk.dtype)
        dv[...] = dv_acc[pl.ds(place, part), :].astype(dv.dtype)


def attention(info, docs, queries, grad_output, prev, own, grad_queries, chunk):
    tokens = queries.shape[0]
    pieces = len(own)
    part = tokens // pieces
    width = own[0].shape[1] // 2
    heads = width // HD
    first = chunk * heads
    wide = pl.BlockSpec((tokens, G * HD), lambda k: (0, first + k))
    key_block = pl.BlockSpec((part, HD), lambda k: (0, k))
    val_block = pl.BlockSpec((part, HD), lambda k: (0, heads + k))
    scalars = pl.BlockSpec(memory_space=pltpu.SMEM)
    count = 2 * pieces
    aliased = grad_queries is not None
    narrow = [jax.ShapeDtypeStruct((part, width), BF16)] * pieces + [
        jax.ShapeDtypeStruct((part, width), F32)
    ] * pieces
    work = 2 * tokens * G * HD * tokens * heads
    outs = pl.pallas_call(
        functools.partial(attn_kernel, tokens=tokens, pieces=pieces, aliased=aliased),
        grid=(heads,),
        in_specs=[scalars, scalars, wide, wide]
        + [key_block] * count
        + [val_block] * count
        + ([pl.BlockSpec(memory_space=pl.ANY)] if aliased else []),
        out_specs=[wide] + [key_block] * (2 * count),
        out_shape=[jax.ShapeDtypeStruct(queries.shape, BF16)] + narrow + narrow,
        scratch_shapes=[pltpu.VMEM((2 * tokens, HD), BF16)] * 2
        + [pltpu.VMEM((2 * tokens, HD), F32)] * 2
        + [
            pltpu.VMEM((tokens // ROW_TILE, tokens + ROW_TILE, ROW_TILE), F32),
            pltpu.SMEM((tokens // ROW_TILE,), jnp.int32),
        ],
        input_output_aliases={4 + 2 * count: 0} if aliased else {},
        compiler_params=pltpu.CompilerParams(vmem_limit_bytes=51 << 20),
        cost_estimate=pl.CostEstimate(
            flops=5 * work, bytes_accessed=3 * tokens * G * HD * 2 * heads, transcendentals=0
        ),
        name="attention",
    )(info, docs, queries, grad_output, *(prev + own) * 2, *([grad_queries] if aliased else []))
    dq, rest = outs[0], outs[1:]
    dk, dv = rest[:count], rest[count:]
    join = lambda i: jnp.concatenate([dk[i], dv[i]], axis=1)
    pair = lambda i: (dk[i], dv[i])
    return dq, [join(i) for i in range(pieces)], [pair(i) for i in range(pieces, count)]


def shift(value, steps):
    count = lax.axis_size("ctx")
    first, last = max(0, -steps), min(count, count - steps)
    return lax.ppermute(value, "ctx", [(i, i + steps) for i in range(first, last)])


def swap(value):
    return lax.ppermute(value, "head", [(0, 1), (1, 0)])


def add(own, arrived):
    return (jnp.concatenate(own, axis=1) + arrived.astype(F32)).astype(BF16)


def per_device(queries, key_rows, value_rows, grad_output, doc_lengths):
    tokens = queries.shape[0]
    head_count = lax.axis_size("head")
    kv_local = KVH // head_count
    local = kv_local * HD
    me = lax.axis_index("head")
    shard = lax.axis_index("ctx")
    chunks = 2 if kv_local % 2 == 0 else 1
    width = local // chunks
    cut = lambda x, start: lax.dynamic_slice_in_dim(x, start, width, axis=1)
    grad_queries = None

    if head_count == 2:
        info = jnp.stack([shard, me * (tokens // 2)]).astype(jnp.int32)
        both = lambda start: jnp.concatenate([cut(key_rows, start), cut(value_rows, start)], axis=1)
        mine = [both(me * local + j * width) for j in range(chunks)]
        recv = [swap(both((1 - me) * local + j * width)) for j in range(chunks)]
        prev = [[shift(mine[0], 1), shift(recv[0], 1)]]
        for j in range(1, chunks):
            arrived = shift(jnp.concatenate([mine[j], recv[j]], axis=0), 1)
            prev.append([arrived[: tokens // 2], arrived[tokens // 2 :]])
        kept, taken = [], []
        for j in range(chunks):
            grad_queries, gone, own = attention(
                info, doc_lengths, queries, grad_output, prev[j], [mine[j], recv[j]], grad_queries, j
            )
            if j < chunks - 1:
                back = shift(jnp.concatenate(gone, axis=0), -1)
                back = [back[: tokens // 2], back[tokens // 2 :]]
            else:
                back = [shift(x, -1) for x in gone]
            taken.append(swap(add(own[1], back[1])))
            kept.append(add(own[0], back[0]))
        outs = []
        for at in range(2):
            here = [x[:, at * width : (at + 1) * width] for x in kept]
            there = [x[:, at * width : (at + 1) * width] for x in taken]
            low = jnp.concatenate([jnp.where(me == 0, a, b) for a, b in zip(here, there)], axis=1)
            high = jnp.concatenate([jnp.where(me == 0, b, a) for a, b in zip(here, there)], axis=1)
            outs.append(jnp.concatenate([low, high], axis=1))
        return (grad_queries, *outs)

    info = jnp.stack([shard, 0 * shard]).astype(jnp.int32)
    key_own = lax.all_to_all(key_rows, "head", split_axis=1, concat_axis=0, tiled=True)
    val_own = lax.all_to_all(value_rows, "head", split_axis=1, concat_axis=0, tiled=True)
    totals = []
    for j in range(chunks):
        own = jnp.concatenate([cut(key_own, j * width), cut(val_own, j * width)], axis=1)
        grad_queries, gone, mine = attention(
            info, doc_lengths, queries, grad_output, [shift(own, 1)], [own], grad_queries, j
        )
        totals.append(add(mine[0], shift(gone[0], -1)))
    outs = []
    for at in range(2):
        total = jnp.concatenate([x[:, at * width : (at + 1) * width] for x in totals], axis=1)
        outs.append(lax.all_to_all(total, "head", split_axis=0, concat_axis=1, tiled=True))
    return (grad_queries, *outs)


def solution(mesh):
    in_specs = (
        P("ctx", "head"),
        P(("ctx", "head"), None),
        P(("ctx", "head"), None),
        P("ctx", "head"),
        P(),
    )
    out_specs = (P("ctx", "head"), P(("ctx", "head"), None), P(("ctx", "head"), None))
    return jax.shard_map(
        per_device, mesh=mesh, in_specs=in_specs, out_specs=out_specs, check_vma=False
    )
```

```python
import functools
import math

import jax
import jax.numpy as jnp
from jax import lax
from jax.experimental import pallas as pl
from jax.experimental.pallas import tpu as pltpu
from jax.sharding import PartitionSpec as P

H = 64
KVH = 8
HD = 128
G = H // KVH
NEG = -1e30
ROW_TILE = 128
KEY_STEP = 128
BF16 = jnp.bfloat16
F32 = jnp.float32
NT = (((1,), (1,)), ((), ()))
NN = (((1,), (0,)), ((), ()))
TN = (((0,), (0,)), ((), ()))


def attn_kernel(info_ref, start_ref, q_ref, do_ref, *refs, tokens, pieces, aliased):
    count = 2 * pieces
    kv_in, refs = refs[:count], refs[count:]
    if aliased:
        refs = refs[1:]
    dq_ref, dkv_out, refs = refs[0], refs[1 : 1 + count], refs[1 + count :]
    k_win, v_win, dk_acc, dv_acc, bias = refs
    rt = ROW_TILE
    n_tiles = tokens // rt
    part = tokens // pieces
    width = kv_in[0].shape[1] // 2
    scale = math.log2(math.e) / math.sqrt(HD)
    factor = 1.0 / math.sqrt(HD)
    base = info_ref[0] * tokens
    first_off = pl.multiple_of(info_ref[1], part)
    if pieces == 1:
        places = [0, tokens]
    else:
        second_off = pl.multiple_of(part - first_off, part)
        places = [first_off, second_off, tokens + first_off, tokens + second_off]
    head = pl.program_id(0)
    k_cols = pl.ds(pl.multiple_of(head * HD, HD), HD)
    v_cols = pl.ds(pl.multiple_of(width + head * HD, HD), HD)

    @pl.when(head == 0)
    def _():
        for r in range(n_tiles):
            cols = slice(r * rt, (r + 1) * rt)
            pos = base + r * rt + lax.broadcasted_iota(jnp.int32, (1, rt), 1)
            key_pos = (
                base + r * rt - tokens + lax.broadcasted_iota(jnp.int32, (tokens + rt, rt), 0)
            )
            ok = (key_pos >= start_ref[:, cols]) & (key_pos <= pos)
            bias[r] = jnp.where(ok, 0.0, NEG).astype(F32)

    for place, kv in zip(places, kv_in):
        k_win[pl.ds(place, part), :] = kv[:, k_cols]
        v_win[pl.ds(place, part), :] = kv[:, v_cols]
    dk_acc[...] = jnp.zeros_like(dk_acc)
    dv_acc[...] = jnp.zeros_like(dv_acc)

    def row_tile(r, _):
        rows = pl.ds(pl.multiple_of(r * rt, rt), rt)
        for span in range(rt, tokens + rt + 1, KEY_STEP):

            @pl.when(info_ref[2 + r] == span)
            def _(span=span):
                over = tokens + rt - span
                window = pl.ds(pl.multiple_of(r * rt + over, KEY_STEP), span)
                k = k_win[window, :]
                v = v_win[window, :]
                mask = jnp.concatenate([bias[r, over:, :]] * G, axis=1)
                heads = [slice(h * HD, (h + 1) * HD) for h in range(G)]
                q = jnp.concatenate([q_ref[rows, s] for s in heads], axis=0)
                do = jnp.concatenate([do_ref[rows, s] for s in heads], axis=0)
                s = lax.dot_general(k, q, NT, preferred_element_type=F32) + mask
                dp = lax.dot_general(v, do, NT, preferred_element_type=F32)
                e = jnp.exp2((s - jnp.max(s, axis=0, keepdims=True)) * scale)
                inv = 1.0 / jnp.sum(e, axis=0, keepdims=True)
                delta = jnp.sum(e * dp, axis=0, keepdims=True) * inv
                p = e * inv
                ds = (p * (dp - delta)).astype(BF16)
                dv_acc[window, :] += lax.dot_general(
                    p.astype(BF16), do, NN, preferred_element_type=F32
                )
                dk_acc[window, :] += lax.dot_general(ds, q, NN, preferred_element_type=F32)
                dq = lax.dot_general(ds, k, TN, preferred_element_type=F32)
                dq = (dq * factor).astype(BF16)
                for h, s in enumerate(heads):
                    dq_ref[rows, s] = dq[h * rt : (h + 1) * rt]

        return 0

    lax.fori_loop(0, n_tiles, row_tile, 0)
    for place, dkv in zip(places, dkv_out):
        dkv[:, k_cols] = (dk_acc[pl.ds(place, part), :] * factor).astype(dkv.dtype)
        dkv[:, v_cols] = dv_acc[pl.ds(place, part), :].astype(dkv.dtype)


def attention(info, start, queries, grad_output, prev, own, grad_queries, chunk):
    tokens = queries.shape[0]
    pieces = len(own)
    part = tokens // pieces
    width = own[0].shape[1] // 2
    heads = width // HD
    first = chunk * heads
    wide = pl.BlockSpec((tokens, G * HD), lambda k: (0, first + k))
    whole = pl.BlockSpec((part, 2 * width), lambda k: (0, 0))
    scalars = pl.BlockSpec(memory_space=pltpu.SMEM)
    count = 2 * pieces
    aliased = grad_queries is not None
    work = 2 * tokens * G * HD * tokens * heads
    outs = pl.pallas_call(
        functools.partial(attn_kernel, tokens=tokens, pieces=pieces, aliased=aliased),
        grid=(heads,),
        in_specs=[scalars, pl.BlockSpec((1, tokens), lambda k: (0, 0)), wide, wide]
        + [whole] * count
        + ([pl.BlockSpec(memory_space=pl.ANY)] if aliased else []),
        out_specs=[wide] + [whole] * count,
        out_shape=[jax.ShapeDtypeStruct(queries.shape, BF16)]
        + [jax.ShapeDtypeStruct((part, 2 * width), BF16)] * pieces
        + [jax.ShapeDtypeStruct((part, 2 * width), F32)] * pieces,
        scratch_shapes=[pltpu.VMEM((2 * tokens, HD), BF16)] * 2
        + [pltpu.VMEM((2 * tokens, HD), F32)] * 2
        + [pltpu.VMEM((tokens // ROW_TILE, tokens + ROW_TILE, ROW_TILE), F32)],
        input_output_aliases={4 + count: 0} if aliased else {},
        compiler_params=pltpu.CompilerParams(vmem_limit_bytes=51 << 20),
        cost_estimate=pl.CostEstimate(
            flops=5 * work, bytes_accessed=3 * tokens * G * HD * 2 * heads, transcendentals=0
        ),
        name="attention",
    )(info, start, queries, grad_output, *prev, *own, *([grad_queries] if aliased else []))
    return outs[0], outs[1 : 1 + pieces], outs[1 + pieces :]


def documents(doc_lengths, shard, tokens, first_off):
    bounds = jnp.cumsum(doc_lengths)
    base = shard * tokens
    pos = base + jnp.arange(tokens, dtype=jnp.int32)
    start = jnp.max(jnp.where(pos[None, :] >= bounds[:, None], bounds[:, None], 0), axis=0)
    ends = base + ROW_TILE * (1 + jnp.arange(tokens // ROW_TILE, dtype=jnp.int32))
    spans = ends - start[::ROW_TILE] // KEY_STEP * KEY_STEP
    info = jnp.concatenate([jnp.stack([shard, first_off]), spans]).astype(jnp.int32)
    return info, start[None, :].astype(jnp.int32)


def shift(value, steps):
    count = lax.axis_size("ctx")
    first, last = max(0, -steps), min(count, count - steps)
    return lax.ppermute(value, "ctx", [(i, i + steps) for i in range(first, last)])


def swap(value):
    return lax.ppermute(value, "head", [(0, 1), (1, 0)])


def add(own, arrived):
    return (own + arrived.astype(F32)).astype(BF16)


def per_device(queries, key_rows, value_rows, grad_output, doc_lengths):
    tokens = queries.shape[0]
    head_count = lax.axis_size("head")
    kv_local = KVH // head_count
    local = kv_local * HD
    me = lax.axis_index("head")
    shard = lax.axis_index("ctx")
    chunks = 2 if kv_local % 2 == 0 else 1
    width = local // chunks
    cut = lambda x, start: lax.dynamic_slice_in_dim(x, start, width, axis=1)
    grad_queries = None

    if head_count == 2:
        half = tokens // 2
        info, start = documents(doc_lengths, shard, tokens, me * half)
        rows = (key_rows, value_rows)
        both = lambda at: jnp.concatenate([cut(x, at) for x in rows], axis=1)
        other = [both((1 - me) * local)]
        mine = [both(me * local + j * width) for j in range(chunks)]
        other += [both((1 - me) * local + j * width) for j in range(1, chunks)]
        recv = [swap(x) for x in other]
        prev = [[shift(mine[0], 1), shift(recv[0], 1)]]
        for j in range(1, chunks):
            arrived = shift(jnp.concatenate([mine[j], recv[j]], axis=0), 1)
            prev.append([arrived[:half], arrived[half:]])
        outs = [jnp.zeros_like(key_rows), jnp.zeros_like(value_rows)]
        earlier = None

        def put(part, at):
            for i in range(2):
                block = part[:, i * width : (i + 1) * width]
                outs[i] = lax.dynamic_update_slice_in_dim(outs[i], block, at, axis=1)

        for j in range(chunks):
            grad_queries, gone, own = attention(
                info, start, queries, grad_output, prev[j], [mine[j], recv[j]], grad_queries, j
            )
            if j < chunks - 1:
                back = shift(jnp.concatenate(gone, axis=0), -1)
                back = [back[:half], back[half:]]
                earlier = add(own[1], back[1])
            else:
                if earlier is not None:
                    put(swap(earlier), (1 - me) * local)
                back = shift(jnp.concatenate(gone, axis=0), -1)
                back = [back[:half], back[half:]]
                last = swap(add(own[1], back[1]))
            put(add(own[0], back[0]), me * local + j * width)
        put(last, (1 - me) * local + (chunks - 1) * width)
        return (grad_queries, *outs)

    info, start = documents(doc_lengths, shard, tokens, 0 * shard)
    key_own = lax.all_to_all(key_rows, "head", split_axis=1, concat_axis=0, tiled=True)
    val_own = lax.all_to_all(value_rows, "head", split_axis=1, concat_axis=0, tiled=True)
    totals = []
    for j in range(chunks):
        own = jnp.concatenate([cut(key_own, j * width), cut(val_own, j * width)], axis=1)
        grad_queries, gone, mine = attention(
            info, start, queries, grad_output, [shift(own, 1)], [own], grad_queries, j
        )
        totals.append(add(mine[0], shift(gone[0], -1)))
    outs = []
    for at in range(2):
        total = jnp.concatenate([x[:, at * width : (at + 1) * width] for x in totals], axis=1)
        outs.append(lax.all_to_all(total, "head", split_axis=0, concat_axis=1, tiled=True))
    return (grad_queries, *outs)


def solution(mesh):
    in_specs = (
        P("ctx", "head"),
        P(("ctx", "head"), None),
        P(("ctx", "head"), None),
        P("ctx", "head"),
        P(),
    )
    out_specs = (P("ctx", "head"), P(("ctx", "head"), None), P(("ctx", "head"), None))
    return jax.shard_map(
        per_device, mesh=mesh, in_specs=in_specs, out_specs=out_specs, check_vma=False
    )
```

```python
import functools
import math

import jax
import jax.numpy as jnp
from jax import lax
from jax.experimental import pallas as pl
from jax.experimental.pallas import tpu as pltpu
from jax.sharding import PartitionSpec as P

H = 64
KVH = 8
HD = 128
G = H // KVH
NEG = -1e30
ROW_TILE = 128
KEY_STEP = 128
BF16 = jnp.bfloat16
F32 = jnp.float32
NT = (((1,), (1,)), ((), ()))
NN = (((1,), (0,)), ((), ()))
TN = (((0,), (0,)), ((), ()))


def attn_kernel(info_ref, start_ref, q_ref, do_ref, *refs, tokens, pieces, aliased, first):
    count = 2 * pieces
    kv_in, refs = refs[:count], refs[count:]
    if aliased:
        refs = refs[1:]
    dq_ref, dkv_out, refs = refs[0], refs[1 : 1 + count], refs[1 + count :]
    k_win, v_win, dk_acc, dv_acc, bias, q_buf, do_buf, dq_buf, sems = refs
    rt = ROW_TILE
    n_tiles = tokens // rt
    part = tokens // pieces
    width = kv_in[0].shape[1] // 2
    scale = math.log2(math.e) / math.sqrt(HD)
    factor = 1.0 / math.sqrt(HD)
    base = info_ref[0] * tokens
    first_off = pl.multiple_of(info_ref[1], part)
    if pieces == 1:
        places = [0, tokens]
    else:
        second_off = pl.multiple_of(part - first_off, part)
        places = [first_off, second_off, tokens + first_off, tokens + second_off]
    head = pl.program_id(0)
    k_cols = pl.ds(pl.multiple_of(head * HD, HD), HD)
    v_cols = pl.ds(pl.multiple_of(width + head * HD, HD), HD)

    heads_here = width // HD

    def copies(h, r):
        rows = pl.ds(r * rt, rt)
        cols = pl.ds(pl.multiple_of((first + h) * G * HD, G * HD), G * HD)
        return (
            pltpu.make_async_copy(q_ref.at[rows, cols], q_buf.at[h, rows, :], sems.at[0, h, r]),
            pltpu.make_async_copy(do_ref.at[rows, cols], do_buf.at[h, rows, :], sems.at[1, h, r]),
            pltpu.make_async_copy(dq_buf.at[h, rows, :], dq_ref.at[rows, cols], sems.at[2, h, r]),
        )

    @pl.when(head == 0)
    def _():
        for h in range(heads_here):
            for r in range(n_tiles):
                get_q, get_do, _ = copies(h, r)
                get_q.start()
                get_do.start()
        for r in range(n_tiles):
            cols = slice(r * rt, (r + 1) * rt)
            pos = base + r * rt + lax.broadcasted_iota(jnp.int32, (1, rt), 1)
            key_pos = (
                base + r * rt - tokens + lax.broadcasted_iota(jnp.int32, (tokens + rt, rt), 0)
            )
            ok = (key_pos >= start_ref[:, cols]) & (key_pos <= pos)
            bias[r] = jnp.where(ok, 0.0, NEG).astype(F32)

    for place, kv in zip(places, kv_in):
        k_win[pl.ds(place, part), :] = kv[:, k_cols]
        v_win[pl.ds(place, part), :] = kv[:, v_cols]
    dk_acc[...] = jnp.zeros_like(dk_acc)
    dv_acc[...] = jnp.zeros_like(dv_acc)

    def row_tile(r, _):
        rows = pl.ds(pl.multiple_of(r * rt, rt), rt)
        get_q, get_do, put_dq = copies(head, r)
        get_q.wait()
        get_do.wait()
        for span in range(rt, tokens + rt + 1, KEY_STEP):

            @pl.when(info_ref[2 + r] == span)
            def _(span=span):
                over = tokens + rt - span
                window = pl.ds(pl.multiple_of(r * rt + over, KEY_STEP), span)
                k = k_win[window, :]
                v = v_win[window, :]
                mask = jnp.concatenate([bias[r, over:, :]] * G, axis=1)
                heads = [slice(h * HD, (h + 1) * HD) for h in range(G)]
                q = jnp.concatenate([q_buf[head, rows, s] for s in heads], axis=0)
                do = jnp.concatenate([do_buf[head, rows, s] for s in heads], axis=0)
                s = lax.dot_general(k, q, NT, preferred_element_type=F32) + mask
                dp = lax.dot_general(v, do, NT, preferred_element_type=F32)
                e = jnp.exp2((s - jnp.max(s, axis=0, keepdims=True)) * scale)
                inv = 1.0 / jnp.sum(e, axis=0, keepdims=True)
                delta = jnp.sum(e * dp, axis=0, keepdims=True) * inv
                p = e * inv
                ds = (p * (dp - delta)).astype(BF16)
                dv_acc[window, :] += lax.dot_general(
                    p.astype(BF16), do, NN, preferred_element_type=F32
                )
                dk_acc[window, :] += lax.dot_general(ds, q, NN, preferred_element_type=F32)
                dq = lax.dot_general(ds, k, TN, preferred_element_type=F32)
                dq = (dq * factor).astype(BF16)
                for h, s in enumerate(heads):
                    dq_buf[head, rows, s] = dq[h * rt : (h + 1) * rt]

        put_dq.start()
        return 0

    lax.fori_loop(0, n_tiles, row_tile, 0)
    for place, dkv in zip(places, dkv_out):
        dkv[:, k_cols] = (dk_acc[pl.ds(place, part), :] * factor).astype(dkv.dtype)
        dkv[:, v_cols] = dv_acc[pl.ds(place, part), :].astype(dkv.dtype)

    @pl.when(head == heads_here - 1)
    def _():
        for h in range(heads_here):
            for r in range(n_tiles):
                copies(h, r)[2].wait()


def attention(info, start, queries, grad_output, prev, own, grad_queries, chunk):
    tokens = queries.shape[0]
    pieces = len(own)
    part = tokens // pieces
    width = own[0].shape[1] // 2
    heads = width // HD
    first = chunk * heads
    n_tiles = tokens // ROW_TILE
    wide = pl.BlockSpec(memory_space=pltpu.HBM)
    whole = pl.BlockSpec((part, 2 * width), lambda k: (0, 0))
    scalars = pl.BlockSpec(memory_space=pltpu.SMEM)
    count = 2 * pieces
    aliased = grad_queries is not None
    work = 2 * tokens * G * HD * tokens * heads
    outs = pl.pallas_call(
        functools.partial(attn_kernel, tokens=tokens, pieces=pieces, aliased=aliased, first=first),
        grid=(heads,),
        in_specs=[scalars, pl.BlockSpec((1, tokens), lambda k: (0, 0)), wide, wide]
        + [whole] * count
        + ([wide] if aliased else []),
        out_specs=[wide] + [whole] * count,
        out_shape=[jax.ShapeDtypeStruct(queries.shape, BF16)]
        + [jax.ShapeDtypeStruct((part, 2 * width), BF16)] * pieces
        + [jax.ShapeDtypeStruct((part, 2 * width), F32)] * pieces,
        scratch_shapes=[pltpu.VMEM((2 * tokens, HD), BF16)] * 2
        + [pltpu.VMEM((2 * tokens, HD), F32)] * 2
        + [pltpu.VMEM((n_tiles, tokens + ROW_TILE, ROW_TILE), F32)]
        + [pltpu.VMEM((heads, tokens, G * HD), BF16)] * 3
        + [pltpu.SemaphoreType.DMA((3, heads, n_tiles))],
        input_output_aliases={4 + count: 0} if aliased else {},
        compiler_params=pltpu.CompilerParams(vmem_limit_bytes=51 << 20),
        cost_estimate=pl.CostEstimate(
            flops=5 * work, bytes_accessed=3 * tokens * G * HD * 2 * heads, transcendentals=0
        ),
        name="attention",
    )(info, start, queries, grad_output, *prev, *own, *([grad_queries] if aliased else []))
    return outs[0], outs[1 : 1 + pieces], outs[1 + pieces :]


def documents(doc_lengths, shard, tokens, first_off):
    bounds = jnp.cumsum(doc_lengths)
    base = shard * tokens
    pos = base + jnp.arange(tokens, dtype=jnp.int32)
    start = jnp.max(jnp.where(pos[None, :] >= bounds[:, None], bounds[:, None], 0), axis=0)
    ends = base + ROW_TILE * (1 + jnp.arange(tokens // ROW_TILE, dtype=jnp.int32))
    spans = ends - start[::ROW_TILE] // KEY_STEP * KEY_STEP
    info = jnp.concatenate([jnp.stack([shard, first_off]), spans]).astype(jnp.int32)
    return info, start[None, :].astype(jnp.int32)


def shift(value, steps):
    count = lax.axis_size("ctx")
    first, last = max(0, -steps), min(count, count - steps)
    return lax.ppermute(value, "ctx", [(i, i + steps) for i in range(first, last)])


def swap(value):
    return lax.ppermute(value, "head", [(0, 1), (1, 0)])


def add(own, arrived):
    return (own + arrived.astype(F32)).astype(BF16)


def per_device(queries, key_rows, value_rows, grad_output, doc_lengths):
    tokens = queries.shape[0]
    head_count = lax.axis_size("head")
    kv_local = KVH // head_count
    local = kv_local * HD
    me = lax.axis_index("head")
    shard = lax.axis_index("ctx")
    chunks = 2 if kv_local % 2 == 0 else 1
    width = local // chunks
    cut = lambda x, start: lax.dynamic_slice_in_dim(x, start, width, axis=1)
    grad_queries = None

    if head_count == 2:
        half = tokens // 2
        info, start = documents(doc_lengths, shard, tokens, me * half)
        rows = (key_rows, value_rows)
        both = lambda at: jnp.concatenate([cut(x, at) for x in rows], axis=1)
        other = [both((1 - me) * local)]
        mine = [both(me * local + j * width) for j in range(chunks)]
        other += [both((1 - me) * local + j * width) for j in range(1, chunks)]
        recv = [swap(x) for x in other]
        prev = [[shift(mine[0], 1), shift(recv[0], 1)]]
        for j in range(1, chunks):
            arrived = shift(jnp.concatenate([mine[j], recv[j]], axis=0), 1)
            prev.append([arrived[:half], arrived[half:]])
        outs = [jnp.zeros_like(key_rows), jnp.zeros_like(value_rows)]
        earlier = None

        def put(part, at):
            for i in range(2):
                block = part[:, i * width : (i + 1) * width]
                outs[i] = lax.dynamic_update_slice_in_dim(outs[i], block, at, axis=1)

        for j in range(chunks):
            grad_queries, gone, own = attention(
                info, start, queries, grad_output, prev[j], [mine[j], recv[j]], grad_queries, j
            )
            if j < chunks - 1:
                back = shift(jnp.concatenate(gone, axis=0), -1)
                back = [back[:half], back[half:]]
                earlier = add(own[1], back[1])
            else:
                if earlier is not None:
                    put(swap(earlier), (1 - me) * local)
                back = shift(jnp.concatenate(gone, axis=0), -1)
                back = [back[:half], back[half:]]
                last = swap(add(own[1], back[1]))
            put(add(own[0], back[0]), me * local + j * width)
        put(last, (1 - me) * local + (chunks - 1) * width)
        return (grad_queries, *outs)

    info, start = documents(doc_lengths, shard, tokens, 0 * shard)
    key_own = lax.all_to_all(key_rows, "head", split_axis=1, concat_axis=0, tiled=True)
    val_own = lax.all_to_all(value_rows, "head", split_axis=1, concat_axis=0, tiled=True)
    totals = []
    for j in range(chunks):
        own = jnp.concatenate([cut(key_own, j * width), cut(val_own, j * width)], axis=1)
        grad_queries, gone, mine = attention(
            info, start, queries, grad_output, [shift(own, 1)], [own], grad_queries, j
        )
        totals.append(add(mine[0], shift(gone[0], -1)))
    outs = []
    for at in range(2):
        total = jnp.concatenate([x[:, at * width : (at + 1) * width] for x in totals], axis=1)
        outs.append(lax.all_to_all(total, "head", split_axis=0, concat_axis=1, tiled=True))
    return (grad_queries, *outs)


def solution(mesh):
    in_specs = (
        P("ctx", "head"),
        P(("ctx", "head"), None),
        P(("ctx", "head"), None),
        P("ctx", "head"),
        P(),
    )
    out_specs = (P("ctx", "head"), P(("ctx", "head"), None), P(("ctx", "head"), None))
    return jax.shard_map(
        per_device, mesh=mesh, in_specs=in_specs, out_specs=out_specs, check_vma=False
    )
```

```python
import functools
import math

import jax
import jax.numpy as jnp
from jax import lax
from jax.experimental import pallas as pl
from jax.experimental.pallas import tpu as pltpu
from jax.sharding import PartitionSpec as P

H = 64
KVH = 8
HD = 128
G = H // KVH
NEG = -1e30
ROW_TILE = 128
KEY_STEP = 64
BF16 = jnp.bfloat16
F32 = jnp.float32
NT = (((1,), (1,)), ((), ()))
NN = (((1,), (0,)), ((), ()))
TN = (((0,), (0,)), ((), ()))


def attn_kernel(info_ref, start_ref, q_ref, do_ref, *refs, tokens, pieces, aliased, first):
    count = 2 * pieces
    kv_in, refs = refs[:count], refs[count:]
    if aliased:
        refs = refs[1:]
    dq_ref, dkv_out, refs = refs[0], refs[1 : 1 + count], refs[1 + count :]
    k_win, v_win, dk_acc, dv_acc, bias, q_buf, do_buf, dq_buf, sems = refs
    rt = ROW_TILE
    n_tiles = tokens // rt
    part = tokens // pieces
    width = kv_in[0].shape[1] // 2
    scale = math.log2(math.e) / math.sqrt(HD)
    factor = 1.0 / math.sqrt(HD)
    base = info_ref[0] * tokens
    first_off = pl.multiple_of(info_ref[1], part)
    if pieces == 1:
        places = [0, tokens]
    else:
        second_off = pl.multiple_of(part - first_off, part)
        places = [first_off, second_off, tokens + first_off, tokens + second_off]
    head = pl.program_id(0)
    k_cols = pl.ds(pl.multiple_of(head * HD, HD), HD)
    v_cols = pl.ds(pl.multiple_of(width + head * HD, HD), HD)

    heads_here = width // HD

    def copies(h, r):
        rows = pl.ds(r * rt, rt)
        cols = pl.ds(pl.multiple_of((first + h) * G * HD, G * HD), G * HD)
        return (
            pltpu.make_async_copy(q_ref.at[rows, cols], q_buf.at[h, rows, :], sems.at[0, h, r]),
            pltpu.make_async_copy(do_ref.at[rows, cols], do_buf.at[h, rows, :], sems.at[1, h, r]),
            pltpu.make_async_copy(dq_buf.at[h, rows, :], dq_ref.at[rows, cols], sems.at[2, h, r]),
        )

    @pl.when(head == 0)
    def _():
        for h in range(heads_here):
            for r in range(n_tiles):
                get_q, get_do, _ = copies(h, r)
                get_q.start()
                get_do.start()
        for r in range(n_tiles):
            cols = slice(r * rt, (r + 1) * rt)
            pos = base + r * rt + lax.broadcasted_iota(jnp.int32, (1, rt), 1)
            key_pos = (
                base + r * rt - tokens + lax.broadcasted_iota(jnp.int32, (tokens + rt, rt), 0)
            )
            ok = (key_pos >= start_ref[:, cols]) & (key_pos <= pos)
            bias[r] = jnp.where(ok, 0.0, NEG).astype(F32)

    for place, kv in zip(places, kv_in):
        k_win[pl.ds(place, part), :] = kv[:, k_cols]
        v_win[pl.ds(place, part), :] = kv[:, v_cols]
    dk_acc[...] = jnp.zeros_like(dk_acc)
    dv_acc[...] = jnp.zeros_like(dv_acc)

    def row_tile(r, _):
        rows = pl.ds(pl.multiple_of(r * rt, rt), rt)
        get_q, get_do, put_dq = copies(head, r)
        get_q.wait()
        get_do.wait()
        for span in range(rt, tokens + rt + 1, KEY_STEP):

            @pl.when(info_ref[2 + r] == span)
            def _(span=span):
                over = tokens + rt - span
                window = pl.ds(pl.multiple_of(r * rt + over, KEY_STEP), span)
                k = k_win[window, :]
                v = v_win[window, :]
                mask = jnp.concatenate([bias[r, over:, :]] * G, axis=1)
                heads = [slice(h * HD, (h + 1) * HD) for h in range(G)]
                q = jnp.concatenate([q_buf[head, rows, s] for s in heads], axis=0)
                do = jnp.concatenate([do_buf[head, rows, s] for s in heads], axis=0)
                s = lax.dot_general(k, q, NT, preferred_element_type=F32) + mask
                dp = lax.dot_general(v, do, NT, preferred_element_type=F32)
                e = jnp.exp2((s - jnp.max(s, axis=0, keepdims=True)) * scale)
                inv = 1.0 / jnp.sum(e, axis=0, keepdims=True)
                delta = jnp.sum(e * dp, axis=0, keepdims=True) * inv
                p = e * inv
                ds = (p * (dp - delta)).astype(BF16)
                dv_acc[window, :] += lax.dot_general(
                    p.astype(BF16), do, NN, preferred_element_type=F32
                )
                dk_acc[window, :] += lax.dot_general(ds, q, NN, preferred_element_type=F32)
                dq = lax.dot_general(ds, k, TN, preferred_element_type=F32)
                dq = (dq * factor).astype(BF16)
                for h, s in enumerate(heads):
                    dq_buf[head, rows, s] = dq[h * rt : (h + 1) * rt]

        put_dq.start()
        return 0

    lax.fori_loop(0, n_tiles, row_tile, 0)
    for place, dkv in zip(places, dkv_out):
        dkv[:, k_cols] = (dk_acc[pl.ds(place, part), :] * factor).astype(dkv.dtype)
        dkv[:, v_cols] = dv_acc[pl.ds(place, part), :].astype(dkv.dtype)

    @pl.when(head == heads_here - 1)
    def _():
        for h in range(heads_here):
            for r in range(n_tiles):
                copies(h, r)[2].wait()


def attention(info, start, queries, grad_output, prev, own, grad_queries, chunk):
    tokens = queries.shape[0]
    pieces = len(own)
    part = tokens // pieces
    width = own[0].shape[1] // 2
    heads = width // HD
    first = chunk * heads
    n_tiles = tokens // ROW_TILE
    wide = pl.BlockSpec(memory_space=pltpu.HBM)
    whole = pl.BlockSpec((part, 2 * width), lambda k: (0, 0))
    scalars = pl.BlockSpec(memory_space=pltpu.SMEM)
    count = 2 * pieces
    aliased = grad_queries is not None
    work = 2 * tokens * G * HD * tokens * heads
    outs = pl.pallas_call(
        functools.partial(attn_kernel, tokens=tokens, pieces=pieces, aliased=aliased, first=first),
        grid=(heads,),
        in_specs=[scalars, pl.BlockSpec((1, tokens), lambda k: (0, 0)), wide, wide]
        + [whole] * count
        + ([wide] if aliased else []),
        out_specs=[wide] + [whole] * count,
        out_shape=[jax.ShapeDtypeStruct(queries.shape, BF16)]
        + [jax.ShapeDtypeStruct((part, 2 * width), BF16)] * pieces
        + [jax.ShapeDtypeStruct((part, 2 * width), F32)] * pieces,
        scratch_shapes=[pltpu.VMEM((2 * tokens, HD), BF16)] * 2
        + [pltpu.VMEM((2 * tokens, HD), F32)] * 2
        + [pltpu.VMEM((n_tiles, tokens + ROW_TILE, ROW_TILE), F32)]
        + [pltpu.VMEM((heads, tokens, G * HD), BF16)] * 3
        + [pltpu.SemaphoreType.DMA((3, heads, n_tiles))],
        input_output_aliases={4 + count: 0} if aliased else {},
        compiler_params=pltpu.CompilerParams(vmem_limit_bytes=51 << 20),
        cost_estimate=pl.CostEstimate(
            flops=5 * work, bytes_accessed=3 * tokens * G * HD * 2 * heads, transcendentals=0
        ),
        name="attention",
    )(info, start, queries, grad_output, *prev, *own, *([grad_queries] if aliased else []))
    return outs[0], outs[1 : 1 + pieces], outs[1 + pieces :]


def documents(doc_lengths, shard, tokens, first_off):
    bounds = jnp.cumsum(doc_lengths)
    base = shard * tokens
    pos = base + jnp.arange(tokens, dtype=jnp.int32)
    start = jnp.max(jnp.where(pos[None, :] >= bounds[:, None], bounds[:, None], 0), axis=0)
    ends = base + ROW_TILE * (1 + jnp.arange(tokens // ROW_TILE, dtype=jnp.int32))
    spans = ends - start[::ROW_TILE] // KEY_STEP * KEY_STEP
    info = jnp.concatenate([jnp.stack([shard, first_off]), spans]).astype(jnp.int32)
    return info, start[None, :].astype(jnp.int32)


def shift(value, steps):
    count = lax.axis_size("ctx")
    first, last = max(0, -steps), min(count, count - steps)
    return lax.ppermute(value, "ctx", [(i, i + steps) for i in range(first, last)])


def swap(value):
    return lax.ppermute(value, "head", [(0, 1), (1, 0)])


def add(own, arrived):
    return (own + arrived.astype(F32)).astype(BF16)


def per_device(queries, key_rows, value_rows, grad_output, doc_lengths):
    tokens = queries.shape[0]
    head_count = lax.axis_size("head")
    kv_local = KVH // head_count
    local = kv_local * HD
    me = lax.axis_index("head")
    shard = lax.axis_index("ctx")
    chunks = 2 if kv_local % 2 == 0 else 1
    width = local // chunks
    cut = lambda x, start: lax.dynamic_slice_in_dim(x, start, width, axis=1)
    grad_queries = None

    if head_count == 2:
        half = tokens // 2
        info, start = documents(doc_lengths, shard, tokens, me * half)
        rows = (key_rows, value_rows)
        both = lambda at: jnp.concatenate([cut(x, at) for x in rows], axis=1)
        other = [both((1 - me) * local)]
        mine = [both(me * local + j * width) for j in range(chunks)]
        other += [both((1 - me) * local + j * width) for j in range(1, chunks)]
        recv = [swap(x) for x in other]
        prev = [[shift(mine[0], 1), shift(recv[0], 1)]]
        for j in range(1, chunks):
            arrived = shift(jnp.concatenate([mine[j], recv[j]], axis=0), 1)
            prev.append([arrived[:half], arrived[half:]])
        outs = [jnp.zeros_like(key_rows), jnp.zeros_like(value_rows)]
        earlier = None

        def put(part, at):
            for i in range(2):
                block = part[:, i * width : (i + 1) * width]
                outs[i] = lax.dynamic_update_slice_in_dim(outs[i], block, at, axis=1)

        for j in range(chunks):
            grad_queries, gone, own = attention(
                info, start, queries, grad_output, prev[j], [mine[j], recv[j]], grad_queries, j
            )
            if j < chunks - 1:
                back = shift(jnp.concatenate(gone, axis=0), -1)
                back = [back[:half], back[half:]]
                earlier = add(own[1], back[1])
            else:
                if earlier is not None:
                    put(swap(earlier), (1 - me) * local)
                back = shift(jnp.concatenate(gone, axis=0), -1)
                back = [back[:half], back[half:]]
                last = swap(add(own[1], back[1]))
            put(add(own[0], back[0]), me * local + j * width)
        put(last, (1 - me) * local + (chunks - 1) * width)
        return (grad_queries, *outs)

    info, start = documents(doc_lengths, shard, tokens, 0 * shard)
    key_own = lax.all_to_all(key_rows, "head", split_axis=1, concat_axis=0, tiled=True)
    val_own = lax.all_to_all(value_rows, "head", split_axis=1, concat_axis=0, tiled=True)
    totals = []
    for j in range(chunks):
        own = jnp.concatenate([cut(key_own, j * width), cut(val_own, j * width)], axis=1)
        grad_queries, gone, mine = attention(
            info, start, queries, grad_output, [shift(own, 1)], [own], grad_queries, j
        )
        totals.append(add(mine[0], shift(gone[0], -1)))
    outs = []
    for at in range(2):
        total = jnp.concatenate([x[:, at * width : (at + 1) * width] for x in totals], axis=1)
        outs.append(lax.all_to_all(total, "head", split_axis=0, concat_axis=1, tiled=True))
    return (grad_queries, *outs)


def solution(mesh):
    in_specs = (
        P("ctx", "head"),
        P(("ctx", "head"), None),
        P(("ctx", "head"), None),
        P("ctx", "head"),
        P(),
    )
    out_specs = (P("ctx", "head"), P(("ctx", "head"), None), P(("ctx", "head"), None))
    return jax.shard_map(
        per_device, mesh=mesh, in_specs=in_specs, out_specs=out_specs, check_vma=False
    )
```

```python
import functools
import math

import jax
import jax.numpy as jnp
from jax import lax
from jax.experimental import pallas as pl
from jax.experimental.pallas import tpu as pltpu
from jax.sharding import PartitionSpec as P

H = 64
KVH = 8
HD = 128
G = H // KVH
NEG = -1e30
ROW_TILE = 128
KEY_STEP = 64
BF16 = jnp.bfloat16
F32 = jnp.float32
NT = (((1,), (1,)), ((), ()))
NN = (((1,), (0,)), ((), ()))
TN = (((0,), (0,)), ((), ()))


def attn_kernel(info_ref, start_ref, q_ref, do_ref, *refs, tokens, pieces, aliased, first):
    count = 2 * pieces
    kv_in, refs = refs[:count], refs[count:]
    if aliased:
        refs = refs[1:]
    dq_ref, dkv_out, refs = refs[0], refs[1 : 1 + count], refs[1 + count :]
    k_win, v_win, dk_acc, dv_acc, bias, q_buf, do_buf, dq_buf, sems = refs
    rt = ROW_TILE
    n_tiles = tokens // rt
    part = tokens // pieces
    width = kv_in[0].shape[1] // 2
    scale = math.log2(math.e) / math.sqrt(HD)
    factor = 1.0 / math.sqrt(HD)
    base = info_ref[0] * tokens
    first_off = pl.multiple_of(info_ref[1], part)
    if pieces == 1:
        places = [0, tokens]
    else:
        second_off = pl.multiple_of(part - first_off, part)
        places = [first_off, second_off, tokens + first_off, tokens + second_off]
    head = pl.program_id(0)
    k_cols = pl.ds(pl.multiple_of(head * HD, HD), HD)
    v_cols = pl.ds(pl.multiple_of(width + head * HD, HD), HD)

    heads_here = width // HD

    def copies(h, r):
        rows = pl.ds(r * rt, rt)
        cols = pl.ds(pl.multiple_of((first + h) * G * HD, G * HD), G * HD)
        return (
            pltpu.make_async_copy(q_ref.at[rows, cols], q_buf.at[h, rows, :], sems.at[0, h, r]),
            pltpu.make_async_copy(do_ref.at[rows, cols], do_buf.at[h, rows, :], sems.at[1, h, r]),
            pltpu.make_async_copy(dq_buf.at[h, rows, :], dq_ref.at[rows, cols], sems.at[2, h, r]),
        )

    @pl.when(head == 0)
    def _():
        for h in range(heads_here):
            for r in range(n_tiles):
                get_q, get_do, _ = copies(h, r)
                get_q.start()
                get_do.start()
        for r in range(n_tiles):
            cols = slice(r * rt, (r + 1) * rt)
            pos = base + r * rt + lax.broadcasted_iota(jnp.int32, (1, rt), 1)
            key_pos = (
                base + r * rt - tokens + lax.broadcasted_iota(jnp.int32, (tokens + rt, rt), 0)
            )
            ok = (key_pos >= start_ref[:, cols]) & (key_pos <= pos)
            bias[r] = jnp.where(ok, 0.0, NEG).astype(F32)

    for place, kv in zip(places, kv_in):
        k_win[pl.ds(place, part), :] = kv[:, k_cols]
        v_win[pl.ds(place, part), :] = kv[:, v_cols]
    dk_acc[...] = jnp.zeros_like(dk_acc)
    dv_acc[...] = jnp.zeros_like(dv_acc)

    def row_tile(r, _):
        rows = pl.ds(pl.multiple_of(r * rt, rt), rt)
        get_q, get_do, put_dq = copies(head, r)
        get_q.wait()
        get_do.wait()
        def tile(span):
            over = tokens + rt - span
            window = pl.ds(pl.multiple_of(r * rt + over, KEY_STEP), span)
            k = k_win[window, :]
            v = v_win[window, :]
            mask = jnp.concatenate([bias[r, over:, :]] * G, axis=1)
            heads = [slice(h * HD, (h + 1) * HD) for h in range(G)]
            q = jnp.concatenate([q_buf[head, rows, s] for s in heads], axis=0)
            do = jnp.concatenate([do_buf[head, rows, s] for s in heads], axis=0)
            s = lax.dot_general(k, q, NT, preferred_element_type=F32) + mask
            dp = lax.dot_general(v, do, NT, preferred_element_type=F32)
            e = jnp.exp2((s - jnp.max(s, axis=0, keepdims=True)) * scale)
            inv = 1.0 / jnp.sum(e, axis=0, keepdims=True)
            delta = jnp.sum(e * dp, axis=0, keepdims=True) * inv
            p = e * inv
            ds = (p * (dp - delta)).astype(BF16)
            dv_acc[window, :] += lax.dot_general(
                p.astype(BF16), do, NN, preferred_element_type=F32
            )
            dk_acc[window, :] += lax.dot_general(ds, q, NN, preferred_element_type=F32)
            dq = lax.dot_general(ds, k, TN, preferred_element_type=F32)
            dq = (dq * factor).astype(BF16)
            for h, s in enumerate(heads):
                dq_buf[head, rows, s] = dq[h * rt : (h + 1) * rt]

        def choose(spans):
            if len(spans) == 1:
                tile(spans[0])
                return 0
            half = len(spans) // 2
            return lax.cond(
                info_ref[2 + r] < spans[half],
                lambda: choose(spans[:half]),
                lambda: choose(spans[half:]),
            )

        choose(list(range(rt, tokens + rt + 1, KEY_STEP)))
        put_dq.start()
        return 0

    lax.fori_loop(0, n_tiles, row_tile, 0)
    for place, dkv in zip(places, dkv_out):
        dkv[:, k_cols] = (dk_acc[pl.ds(place, part), :] * factor).astype(dkv.dtype)
        dkv[:, v_cols] = dv_acc[pl.ds(place, part), :].astype(dkv.dtype)

    @pl.when(head == heads_here - 1)
    def _():
        for h in range(heads_here):
            for r in range(n_tiles):
                copies(h, r)[2].wait()


def attention(info, start, queries, grad_output, prev, own, grad_queries, chunk):
    tokens = queries.shape[0]
    pieces = len(own)
    part = tokens // pieces
    width = own[0].shape[1] // 2
    heads = width // HD
    first = chunk * heads
    n_tiles = tokens // ROW_TILE
    wide = pl.BlockSpec(memory_space=pltpu.HBM)
    whole = pl.BlockSpec((part, 2 * width), lambda k: (0, 0))
    scalars = pl.BlockSpec(memory_space=pltpu.SMEM)
    count = 2 * pieces
    aliased = grad_queries is not None
    work = 2 * tokens * G * HD * tokens * heads
    outs = pl.pallas_call(
        functools.partial(attn_kernel, tokens=tokens, pieces=pieces, aliased=aliased, first=first),
        grid=(heads,),
        in_specs=[scalars, pl.BlockSpec((1, tokens), lambda k: (0, 0)), wide, wide]
        + [whole] * count
        + ([wide] if aliased else []),
        out_specs=[wide] + [whole] * count,
        out_shape=[jax.ShapeDtypeStruct(queries.shape, BF16)]
        + [jax.ShapeDtypeStruct((part, 2 * width), BF16)] * pieces
        + [jax.ShapeDtypeStruct((part, 2 * width), F32)] * pieces,
        scratch_shapes=[pltpu.VMEM((2 * tokens, HD), BF16)] * 2
        + [pltpu.VMEM((2 * tokens, HD), F32)] * 2
        + [pltpu.VMEM((n_tiles, tokens + ROW_TILE, ROW_TILE), F32)]
        + [pltpu.VMEM((heads, tokens, G * HD), BF16)] * 3
        + [pltpu.SemaphoreType.DMA((3, heads, n_tiles))],
        input_output_aliases={4 + count: 0} if aliased else {},
        compiler_params=pltpu.CompilerParams(vmem_limit_bytes=51 << 20),
        cost_estimate=pl.CostEstimate(
            flops=5 * work, bytes_accessed=3 * tokens * G * HD * 2 * heads, transcendentals=0
        ),
        name="attention",
    )(info, start, queries, grad_output, *prev, *own, *([grad_queries] if aliased else []))
    return outs[0], outs[1 : 1 + pieces], outs[1 + pieces :]


def documents(doc_lengths, shard, tokens, first_off):
    bounds = jnp.cumsum(doc_lengths)
    base = shard * tokens
    pos = base + jnp.arange(tokens, dtype=jnp.int32)
    start = jnp.max(jnp.where(pos[None, :] >= bounds[:, None], bounds[:, None], 0), axis=0)
    ends = base + ROW_TILE * (1 + jnp.arange(tokens // ROW_TILE, dtype=jnp.int32))
    spans = ends - start[::ROW_TILE] // KEY_STEP * KEY_STEP
    info = jnp.concatenate([jnp.stack([shard, first_off]), spans]).astype(jnp.int32)
    return info, start[None, :].astype(jnp.int32)


def shift(value, steps):
    count = lax.axis_size("ctx")
    first, last = max(0, -steps), min(count, count - steps)
    return lax.ppermute(value, "ctx", [(i, i + steps) for i in range(first, last)])


def swap(value):
    return lax.ppermute(value, "head", [(0, 1), (1, 0)])


def add(own, arrived):
    return (own + arrived.astype(F32)).astype(BF16)


def per_device(queries, key_rows, value_rows, grad_output, doc_lengths):
    tokens = queries.shape[0]
    head_count = lax.axis_size("head")
    kv_local = KVH // head_count
    local = kv_local * HD
    me = lax.axis_index("head")
    shard = lax.axis_index("ctx")
    chunks = 2 if kv_local % 2 == 0 else 1
    width = local // chunks
    cut = lambda x, start: lax.dynamic_slice_in_dim(x, start, width, axis=1)
    grad_queries = None

    if head_count == 2:
        half = tokens // 2
        info, start = documents(doc_lengths, shard, tokens, me * half)
        rows = (key_rows, value_rows)
        both = lambda at: jnp.concatenate([cut(x, at) for x in rows], axis=1)
        other = [both((1 - me) * local)]
        mine = [both(me * local + j * width) for j in range(chunks)]
        other += [both((1 - me) * local + j * width) for j in range(1, chunks)]
        recv = [swap(x) for x in other]
        prev = [[shift(mine[0], 1), shift(recv[0], 1)]]
        for j in range(1, chunks):
            arrived = shift(jnp.concatenate([mine[j], recv[j]], axis=0), 1)
            prev.append([arrived[:half], arrived[half:]])
        outs = [jnp.zeros_like(key_rows), jnp.zeros_like(value_rows)]
        earlier = None

        def put(part, at):
            for i in range(2):
                block = part[:, i * width : (i + 1) * width]
                outs[i] = lax.dynamic_update_slice_in_dim(outs[i], block, at, axis=1)

        for j in range(chunks):
            grad_queries, gone, own = attention(
                info, start, queries, grad_output, prev[j], [mine[j], recv[j]], grad_queries, j
            )
            if j < chunks - 1:
                back = shift(jnp.concatenate(gone, axis=0), -1)
                back = [back[:half], back[half:]]
                earlier = add(own[1], back[1])
            else:
                if earlier is not None:
                    put(swap(earlier), (1 - me) * local)
                back = shift(jnp.concatenate(gone, axis=0), -1)
                back = [back[:half], back[half:]]
                last = swap(add(own[1], back[1]))
            put(add(own[0], back[0]), me * local + j * width)
        put(last, (1 - me) * local + (chunks - 1) * width)
        return (grad_queries, *outs)

    info, start = documents(doc_lengths, shard, tokens, 0 * shard)
    key_own = lax.all_to_all(key_rows, "head", split_axis=1, concat_axis=0, tiled=True)
    val_own = lax.all_to_all(value_rows, "head", split_axis=1, concat_axis=0, tiled=True)
    totals = []
    for j in range(chunks):
        own = jnp.concatenate([cut(key_own, j * width), cut(val_own, j * width)], axis=1)
        grad_queries, gone, mine = attention(
            info, start, queries, grad_output, [shift(own, 1)], [own], grad_queries, j
        )
        totals.append(add(mine[0], shift(gone[0], -1)))
    outs = []
    for at in range(2):
        total = jnp.concatenate([x[:, at * width : (at + 1) * width] for x in totals], axis=1)
        outs.append(lax.all_to_all(total, "head", split_axis=0, concat_axis=1, tiled=True))
    return (grad_queries, *outs)


def solution(mesh):
    in_specs = (
        P("ctx", "head"),
        P(("ctx", "head"), None),
        P(("ctx", "head"), None),
        P("ctx", "head"),
        P(),
    )
    out_specs = (P("ctx", "head"), P(("ctx", "head"), None), P(("ctx", "head"), None))
    return jax.shard_map(
        per_device, mesh=mesh, in_specs=in_specs, out_specs=out_specs, check_vma=False
    )
```

```python
import functools
import math

import jax
import jax.numpy as jnp
from jax import lax
from jax.experimental import pallas as pl
from jax.experimental.pallas import tpu as pltpu
from jax.sharding import PartitionSpec as P

H = 64
KVH = 8
HD = 128
G = H // KVH
NEG = -1e30
ROW_TILE = 128
KEY_STEP = 64
BF16 = jnp.bfloat16
F32 = jnp.float32
NT = (((1,), (1,)), ((), ()))
NN = (((1,), (0,)), ((), ()))
TN = (((0,), (0,)), ((), ()))


def attn_kernel(info_ref, start_ref, q_ref, do_ref, *refs, tokens, pieces, aliased, first):
    count = 2 * pieces
    kv_in, refs = refs[:count], refs[count:]
    if aliased:
        refs = refs[1:]
    dq_ref, dkv_out, refs = refs[0], refs[1 : 1 + count], refs[1 + count :]
    k_win, v_win, dk_acc, dv_acc, bias, q_buf, do_buf, dq_buf, sems = refs
    rt = ROW_TILE
    n_tiles = tokens // rt
    part = tokens // pieces
    width = kv_in[0].shape[1] // 2
    scale = math.log2(math.e) / math.sqrt(HD)
    factor = 1.0 / math.sqrt(HD)
    base = info_ref[0] * tokens
    first_off = pl.multiple_of(info_ref[1], part)
    if pieces == 1:
        places = [0, tokens]
    else:
        second_off = pl.multiple_of(part - first_off, part)
        places = [first_off, second_off, tokens + first_off, tokens + second_off]
    head = pl.program_id(0)
    k_cols = pl.ds(pl.multiple_of(head * HD, HD), HD)
    v_cols = pl.ds(pl.multiple_of(width + head * HD, HD), HD)

    heads_here = width // HD

    def copies(h, r):
        rows = pl.ds(r * rt, rt)
        cols = pl.ds(pl.multiple_of((first + h) * G * HD, G * HD), G * HD)
        return (
            pltpu.make_async_copy(q_ref.at[rows, cols], q_buf.at[h, rows, :], sems.at[0, h, r]),
            pltpu.make_async_copy(do_ref.at[rows, cols], do_buf.at[h, rows, :], sems.at[1, h, r]),
            pltpu.make_async_copy(dq_buf.at[h, rows, :], dq_ref.at[rows, cols], sems.at[2, h, r]),
        )

    @pl.when(head == 0)
    def _():
        for h in range(heads_here):
            for r in range(n_tiles):
                get_q, get_do, _ = copies(h, r)
                get_q.start()
                get_do.start()
        for r in range(n_tiles):
            cols = slice(r * rt, (r + 1) * rt)
            pos = base + r * rt + lax.broadcasted_iota(jnp.int32, (1, rt), 1)
            key_pos = (
                base + r * rt - tokens + lax.broadcasted_iota(jnp.int32, (tokens + rt, rt), 0)
            )
            ok = (key_pos >= start_ref[:, cols]) & (key_pos <= pos)
            bias[r] = jnp.where(ok, 0.0, NEG).astype(F32)

    for place, kv in zip(places, kv_in):
        k_win[pl.ds(place, part), :] = kv[:, k_cols]
        v_win[pl.ds(place, part), :] = kv[:, v_cols]
    dk_acc[...] = jnp.zeros_like(dk_acc)
    dv_acc[...] = jnp.zeros_like(dv_acc)

    def row_tile(r, _):
        rows = pl.ds(pl.multiple_of(r * rt, rt), rt)
        get_q, get_do, put_dq = copies(head, r)
        get_q.wait()
        get_do.wait()
        def tile(span):
            over = tokens + rt - span
            window = pl.ds(pl.multiple_of(r * rt + over, KEY_STEP), span)
            k = k_win[window, :]
            v = v_win[window, :]
            mask = jnp.concatenate([bias[r, over:, :]] * G, axis=1)
            heads = [slice(h * HD, (h + 1) * HD) for h in range(G)]
            q = jnp.concatenate([q_buf[head, rows, s] for s in heads], axis=0)
            do = jnp.concatenate([do_buf[head, rows, s] for s in heads], axis=0)
            s = lax.dot_general(k, q, NT, preferred_element_type=F32) + mask
            dp = lax.dot_general(v, do, NT, preferred_element_type=F32)
            e = jnp.exp2((s - jnp.max(s, axis=0, keepdims=True)) * scale)
            inv = 1.0 / jnp.sum(e, axis=0, keepdims=True)
            delta = jnp.sum(e * dp, axis=0, keepdims=True) * inv
            p = e * inv
            ds = (p * (dp - delta)).astype(BF16)
            dv_acc[window, :] += lax.dot_general(
                p.astype(BF16), do, NN, preferred_element_type=F32
            )
            dk_acc[window, :] += lax.dot_general(ds, q, NN, preferred_element_type=F32)
            dq = lax.dot_general(ds, k, TN, preferred_element_type=F32)
            dq = (dq * factor).astype(BF16)
            for h, s in enumerate(heads):
                dq_buf[head, rows, s] = dq[h * rt : (h + 1) * rt]

        def choose(spans):
            if len(spans) == 1:
                tile(spans[0])
                return 0
            half = len(spans) // 2
            return lax.cond(
                info_ref[2 + r] < spans[half],
                lambda: choose(spans[:half]),
                lambda: choose(spans[half:]),
            )

        choose(list(range(rt, tokens + rt + 1, KEY_STEP)))
        put_dq.start()
        return 0

    lax.fori_loop(0, n_tiles, row_tile, 0)
    for place, dkv in zip(places, dkv_out):
        dkv[:, k_cols] = (dk_acc[pl.ds(place, part), :] * factor).astype(dkv.dtype)
        dkv[:, v_cols] = dv_acc[pl.ds(place, part), :].astype(dkv.dtype)

    @pl.when(head == heads_here - 1)
    def _():
        for h in range(heads_here):
            for r in range(n_tiles):
                copies(h, r)[2].wait()


def attention(info, start, queries, grad_output, prev, own, grad_queries, chunk):
    tokens = queries.shape[0]
    pieces = len(own)
    part = tokens // pieces
    width = own[0].shape[1] // 2
    heads = width // HD
    first = chunk * heads
    n_tiles = tokens // ROW_TILE
    wide = pl.BlockSpec(memory_space=pltpu.HBM)
    whole = pl.BlockSpec((part, 2 * width), lambda k: (0, 0))
    scalars = pl.BlockSpec(memory_space=pltpu.SMEM)
    count = 2 * pieces
    aliased = grad_queries is not None
    work = 2 * tokens * G * HD * tokens * heads
    outs = pl.pallas_call(
        functools.partial(attn_kernel, tokens=tokens, pieces=pieces, aliased=aliased, first=first),
        grid=(heads,),
        in_specs=[scalars, pl.BlockSpec((1, tokens), lambda k: (0, 0)), wide, wide]
        + [whole] * count
        + ([wide] if aliased else []),
        out_specs=[wide] + [whole] * count,
        out_shape=[jax.ShapeDtypeStruct(queries.shape, BF16)]
        + [jax.ShapeDtypeStruct((part, 2 * width), BF16)] * pieces
        + [jax.ShapeDtypeStruct((part, 2 * width), F32)] * pieces,
        scratch_shapes=[pltpu.VMEM((2 * tokens, HD), BF16)] * 2
        + [pltpu.VMEM((2 * tokens, HD), F32)] * 2
        + [pltpu.VMEM((n_tiles, tokens + ROW_TILE, ROW_TILE), F32)]
        + [pltpu.VMEM((heads, tokens, G * HD), BF16)] * 3
        + [pltpu.SemaphoreType.DMA((3, heads, n_tiles))],
        input_output_aliases={4 + count: 0} if aliased else {},
        compiler_params=pltpu.CompilerParams(vmem_limit_bytes=51 << 20),
        cost_estimate=pl.CostEstimate(
            flops=5 * work, bytes_accessed=3 * tokens * G * HD * 2 * heads, transcendentals=0
        ),
        name="attention",
    )(info, start, queries, grad_output, *prev, *own, *([grad_queries] if aliased else []))
    return outs[0], outs[1 : 1 + pieces], outs[1 + pieces :]


def documents(doc_lengths, shard, tokens, first_off):
    bounds = jnp.cumsum(doc_lengths)
    base = shard * tokens
    pos = base + jnp.arange(tokens, dtype=jnp.int32)
    start = jnp.max(jnp.where(pos[None, :] >= bounds[:, None], bounds[:, None], 0), axis=0)
    ends = base + ROW_TILE * (1 + jnp.arange(tokens // ROW_TILE, dtype=jnp.int32))
    spans = ends - start[::ROW_TILE] // KEY_STEP * KEY_STEP
    info = jnp.concatenate([jnp.stack([shard, first_off]), spans]).astype(jnp.int32)
    return info, start[None, :].astype(jnp.int32)


def shift(value, steps):
    count = lax.axis_size("ctx")
    first, last = max(0, -steps), min(count, count - steps)
    return lax.ppermute(value, "ctx", [(i, i + steps) for i in range(first, last)])


def swap(value):
    return lax.ppermute(value, "head", [(0, 1), (1, 0)])


def add(own, arrived):
    return (own + arrived.astype(F32)).astype(BF16)


def per_device(queries, key_rows, value_rows, grad_output, doc_lengths):
    tokens = queries.shape[0]
    head_count = lax.axis_size("head")
    kv_local = KVH // head_count
    local = kv_local * HD
    me = lax.axis_index("head")
    shard = lax.axis_index("ctx")
    chunks = 2 if kv_local % 2 == 0 else 1
    width = local // chunks
    cut = lambda x, start: lax.dynamic_slice_in_dim(x, start, width, axis=1)
    pick = lambda x, low, high: jnp.where(me == 0, x[:, low : low + width], x[:, high : high + width])
    grad_queries = None

    if head_count == 2:
        half = tokens // 2
        info, start = documents(doc_lengths, shard, tokens, me * half)
        rows = (key_rows, value_rows)
        both = lambda low, high: jnp.concatenate([pick(x, low, high) for x in rows], axis=1)
        other = [both(local, 0)]
        mine = [both(j * width, local + j * width) for j in range(chunks)]
        other += [both(local + j * width, j * width) for j in range(1, chunks)]
        recv = [swap(x) for x in other]
        prev = [[shift(mine[0], 1), shift(recv[0], 1)]]
        for j in range(1, chunks):
            arrived = shift(jnp.concatenate([mine[j], recv[j]], axis=0), 1)
            prev.append([arrived[:half], arrived[half:]])
        outs = [jnp.zeros_like(key_rows), jnp.zeros_like(value_rows)]
        earlier = None

        def put(part, at):
            for i in range(2):
                block = part[:, i * width : (i + 1) * width]
                outs[i] = lax.dynamic_update_slice_in_dim(outs[i], block, at, axis=1)

        for j in range(chunks):
            grad_queries, gone, own = attention(
                info, start, queries, grad_output, prev[j], [mine[j], recv[j]], grad_queries, j
            )
            if j < chunks - 1:
                back = shift(jnp.concatenate(gone, axis=0), -1)
                back = [back[:half], back[half:]]
                earlier = add(own[1], back[1])
            else:
                if earlier is not None:
                    put(swap(earlier), (1 - me) * local)
                back = shift(jnp.concatenate(gone, axis=0), -1)
                back = [back[:half], back[half:]]
                last = swap(add(own[1], back[1]))
            put(add(own[0], back[0]), me * local + j * width)
        put(last, (1 - me) * local + (chunks - 1) * width)
        return (grad_queries, *outs)

    info, start = documents(doc_lengths, shard, tokens, 0 * shard)
    key_own = lax.all_to_all(key_rows, "head", split_axis=1, concat_axis=0, tiled=True)
    val_own = lax.all_to_all(value_rows, "head", split_axis=1, concat_axis=0, tiled=True)
    totals = []
    for j in range(chunks):
        own = jnp.concatenate([cut(key_own, j * width), cut(val_own, j * width)], axis=1)
        grad_queries, gone, mine = attention(
            info, start, queries, grad_output, [shift(own, 1)], [own], grad_queries, j
        )
        totals.append(add(mine[0], shift(gone[0], -1)))
    outs = []
    for at in range(2):
        total = jnp.concatenate([x[:, at * width : (at + 1) * width] for x in totals], axis=1)
        outs.append(lax.all_to_all(total, "head", split_axis=0, concat_axis=1, tiled=True))
    return (grad_queries, *outs)


def solution(mesh):
    in_specs = (
        P("ctx", "head"),
        P(("ctx", "head"), None),
        P(("ctx", "head"), None),
        P("ctx", "head"),
        P(),
    )
    out_specs = (P("ctx", "head"), P(("ctx", "head"), None), P(("ctx", "head"), None))
    return jax.shard_map(
        per_device, mesh=mesh, in_specs=in_specs, out_specs=out_specs, check_vma=False
    )
```
